32 devices in a mesh: day: 2 (over x), sta: 16 (over z, y, core).
Axes of the slice: x: 2, y: 2, z: 4, core: 2. Of those that a mesh axis runs over, the one named last changes fastest.
Arguments:
- spectra: bfloat16 [256, 4, 2, 8192], P(('day', 'sta')), parts along dimension 0, may hold values from -6 to 6
- window_mask: int32 [256, 4], P(('day', 'sta')), parts along dimension 0, may hold values from 0 to 1, as said below
- pair_slots: int32 [32, 2], P('sta'), may hold values from -1 to 15, as said below
Outputs:
- stacks: bfloat16 [64, 8, 8, 1024], P(('day', 'sta')), parts along dimension 0
The draws below stay inside these ranges and needn't reach their ends.
There are 2 independent parts, one for each index of `day`. The reference program is written for one: setup_inputs(seed, part) draws one part's arguments, and reference() takes and returns one part's arrays. A program takes and returns all parts, laid end to end along the dimension named above; an argument that names none is the same for every part. Nothing has to cross between parts.
Inputs may be any that keep to these rules, and one draw needn't show every extreme that they name: `pair_slots`: row o * 2 + c is slot c of owner block o: either (-1, -1), an empty slot, or two blocks a <= b, each within 2 blocks of o. An owner's live slots come before its empty ones; some owner fills all 2 slots and some owner has none. `window_mask`: in every draw some stations have no valid window at all.
All inputs are finite; a program needn't handle non-finite values.
Results may differ from the reference program's by a relative error of at most 0.0047.
Values may be sent and summed in bfloat16 or wider, within the bound.
A program may use at most 128 MiB of HBM per device.

```python
import math
import jax
import jax.numpy as jnp
from jax import lax

STA_DEV = 8
WINDOWS = 4
FREQS = 8192
LAGS = 1024
CAP = 2
REACH = 2
NBLOCKS = 16
STATIONS = 128
TOTAL_PAIR_SLOTS = 32


def draw_window_mask(key, part):
    keys = jax.random.split(jax.random.fold_in(key, 11), 4)
    valid = (jax.random.randint(keys[0], (STATIONS, WINDOWS), 0, 4) < 3).astype(jnp.int32)
    dead_pick = jax.random.randint(keys[1], (NBLOCKS,), 0, STA_DEV)
    dead_block = jax.random.randint(keys[2], (NBLOCKS,), 0, 2) == 1
    forced_block = jax.random.randint(keys[3], (), 0, NBLOCKS)
    dead_block = dead_block | (jnp.arange(NBLOCKS, dtype=jnp.int32) == forced_block)
    station_in_block = jnp.arange(STA_DEV, dtype=jnp.int32)[None, :]
    silent = (station_in_block == dead_pick[:, None]) & dead_block[:, None]
    silent = silent.reshape(STATIONS)
    return jnp.where(silent[:, None], 0, valid).astype(jnp.int32)


def draw_pair_slots(key, part):
    keys = jax.random.split(jax.random.fold_in(key, 7), 5)
    owners = jnp.arange(NBLOCKS, dtype=jnp.int32)
    active_count = jax.random.randint(keys[0], (NBLOCKS,), 0, CAP + 1)
    busiest = jax.random.randint(keys[1], (), 0, NBLOCKS)
    spare_owner = jax.random.randint(keys[2], (), 0, NBLOCKS - 1)
    spare_owner = jnp.where(spare_owner == busiest, (spare_owner + 1) % (NBLOCKS - 1), spare_owner)
    active_count = jnp.where(owners == busiest, CAP, active_count)
    active_count = jnp.where(owners == spare_owner, 0, active_count)
    active_count = jnp.where(owners == NBLOCKS - 1, jnp.maximum(active_count, 1), active_count)
    first_step = jax.random.randint(keys[3], (NBLOCKS, CAP), -REACH, REACH + 1)
    second_step = jax.random.randint(keys[4], (NBLOCKS, CAP), -REACH, REACH + 1)
    slot_index = jnp.arange(CAP, dtype=jnp.int32)[None, :]
    forced = (owners[:, None] == NBLOCKS - 1) & (slot_index == 0)
    second_step = jnp.where(forced, jnp.maximum(second_step, 0), second_step)
    first_block = jnp.clip(owners[:, None] + first_step, 0, NBLOCKS - 1)
    second_block = jnp.clip(owners[:, None] + second_step, 0, NBLOCKS - 1)
    lower_station_block = jnp.minimum(first_block, second_block)
    upper_station_block = jnp.maximum(first_block, second_block)
    is_live = slot_index < active_count[:, None]
    lower_station_block = jnp.where(is_live, lower_station_block, -1)
    upper_station_block = jnp.where(is_live, upper_station_block, -1)
    return jnp.stack([lower_station_block, upper_station_block], axis=-1).reshape(TOTAL_PAIR_SLOTS, 2).astype(jnp.int32)


def shard_levels(stream_key, shape, pieces, low, high):
    level, own = 1.0, jax.random.fold_in(stream_key, 6)
    for axis_at, shards_of in pieces:
        steps = jnp.exp(jax.random.uniform(jax.random.fold_in(own, axis_at), (shards_of,), jnp.float32, low / len(pieces), high / len(pieces)))
        level = level * jnp.repeat(steps, shape[axis_at] // shards_of).reshape([-1 if axis == axis_at else 1 for axis in range(len(shape))])
    return level


def normal_values(stream_key, shape, scale, limit, cuts=(), kind=jnp.bfloat16):
    array = scale * jax.random.normal(stream_key, shape, jnp.float32)
    if cuts:
        array = array * shard_levels(stream_key, shape, cuts, -0.22, 0.18)
    return jnp.clip(array, -limit, limit).astype(kind)


def setup_inputs(seed: int = 0, part: int = 0) -> dict:
    key_of = jax.random.split(jax.random.key(seed), 4)
    part_splits = jax.random.split(jax.random.fold_in(key_of[3], part), 4)
    return {
        "spectra": normal_values(part_splits[0], (STATIONS, WINDOWS, 2, FREQS), 1.0, 6.0, ((0, 16),)),
        "window_mask": draw_window_mask(jax.random.fold_in(jax.random.fold_in(key_of[3], part), 71), part),
        "pair_slots": draw_pair_slots(jax.random.fold_in(key_of[3], 71), part),
    }


def lag_table(leading_frequency, freq_count, frequency_values, lag_count):
    freq_index = leading_frequency + jnp.arange(freq_count, dtype=jnp.int32)
    lag_index = jnp.arange(lag_count, dtype=jnp.int32) - lag_count // 2
    phase_index = jnp.mod(freq_index[:, None] * lag_index[None, :], 2 * frequency_values)
    phase_angle = phase_index.astype(jnp.float32) * (math.pi / frequency_values)
    return jnp.stack([jnp.cos(phase_angle), -jnp.sin(phase_angle)], axis=0).astype(jnp.bfloat16)

def cross_spectrum(first_real, first_imag, second_real, second_imag):
    real_part = jnp.einsum('pwf,qwf->pqf', first_real, second_real) + jnp.einsum('pwf,qwf->pqf', first_imag, second_imag)
    imag_part = jnp.einsum('pwf,qwf->pqf', first_imag, second_real) - jnp.einsum('pwf,qwf->pqf', first_real, second_imag)
    return jnp.stack([real_part, imag_part], axis=2)

def reference(spectra, window_mask, pair_slots):
    blocks = spectra.reshape(NBLOCKS, STA_DEV, WINDOWS, 2, FREQS)
    block_masks = window_mask.reshape(NBLOCKS, STA_DEV, WINDOWS).astype(jnp.float32)
    lag_rows = lag_table(0, FREQS, FREQS, LAGS).astype(jnp.float32)

    def one_slot(pair_row):
        first_block = jnp.clip(pair_row[0], 0, NBLOCKS - 1).astype(jnp.int32)
        second_block = jnp.clip(pair_row[1], 0, NBLOCKS - 1).astype(jnp.int32)
        is_live = (pair_row[0] >= 0).astype(jnp.float32)
        first_mask = block_masks[first_block]
        second_mask = block_masks[second_block]
        first_spec = blocks[first_block].astype(jnp.float32)
        second_spectrum_rows = blocks[second_block].astype(jnp.float32)
        cross_spec = cross_spectrum(first_spec[:, :, 0] * first_mask[:, :, None], first_spec[:, :, 1] * first_mask[:, :, None], second_spectrum_rows[:, :, 0] * second_mask[:, :, None], second_spectrum_rows[:, :, 1] * second_mask[:, :, None]) * is_live
        cross_spec = lax.optimization_barrier(cross_spec.astype(jnp.bfloat16)).astype(jnp.float32)
        running = jnp.einsum('pqcf,cfl->pql', cross_spec, lag_rows)
        pair_counts = jnp.dot(first_mask.astype(jnp.bfloat16), second_mask.astype(jnp.bfloat16).T, preferred_element_type=jnp.float32)
        weight_scale = 1.0 / (math.sqrt(FREQS) * jnp.maximum(pair_counts, 1.0))
        return (running * weight_scale[:, :, None]).astype(jnp.bfloat16)
    return lax.map(one_slot, pair_slots)
```

```python
import functools
import math

import jax
import jax.numpy as jnp
import numpy as np
from jax import lax
from jax.experimental import pallas as pl
from jax.experimental.pallas import tpu as pltpu
from jax.sharding import PartitionSpec as P

LAGS = 1024
REACH = 2
GROUP = 4
CHUNKS = 4
LANES = 128
FINE = 32
MESH = pl.DeviceIdType.MESH


def phase_tables(steps, frequency_values, lag_count):
    lag = np.arange(lag_count, dtype=np.int64) - lag_count // 2
    phase = np.mod(np.asarray(steps, np.int64)[:, None] * lag[None, :], 2 * frequency_values)
    angle = phase.astype(np.float64) * (math.pi / frequency_values)
    return np.stack([np.cos(angle), np.sin(angle)]).astype(np.float32)


def kernel(
    dims,
    spec_ref,
    mask_ref,
    pair_ref,
    rank_table,
    coarse_table,
    fine_table,
    out_ref,
    held,
    meta,
    slot_smem,
    wide,
    cross,
    table,
    total,
    from_core,
    to_row,
    from_row,
    local_sem,
    group_send,
    group_recv,
    line_send,
    line_recv,
    meta_send,
    meta_recv,
    meta_line_send,
    meta_line_recv,
    sum_send,
    sum_recv,
):
    stations, windows, slots, freqs, lags, groups = dims
    rows = stations * windows * 2
    per_station = windows * 2
    pairs = stations * stations
    held_blocks = GROUP + 2 * REACH
    share = freqs // GROUP
    chunk = share // CHUNKS
    tiles = chunk // LANES

    me = lax.axis_index("sta")
    group = me // GROUP
    rank = me % GROUP
    core = rank % 2
    side = rank // 2
    first = group * GROUP
    has_before = group > 0
    has_behind = group < groups - 1
    before = me - GROUP
    behind = me + GROUP

    barrier = pltpu.get_barrier_semaphore()
    for step in range(1, GROUP):
        pl.semaphore_signal(
            barrier, inc=1, device_id={"sta": first + (rank + step) % GROUP}, device_id_type=MESH
        )

    @pl.when(has_before)
    def _():
        pl.semaphore_signal(barrier, inc=1, device_id={"sta": before}, device_id_type=MESH)

    @pl.when(has_behind)
    def _():
        pl.semaphore_signal(barrier, inc=1, device_id={"sta": behind}, device_id_type=MESH)

    own = REACH + rank
    lane = lax.broadcasted_iota(jnp.int32, (8, LANES), 1)
    slot_row = jnp.zeros((8, LANES), jnp.int32)
    for slot in range(slots):
        for end in range(2):
            slot_row = jnp.where(lane == slot * 2 + end, pair_ref[slot, end], slot_row)
    meta[own, pl.ds(stations, 8), :] = slot_row
    meta[own, pl.ds(0, stations), :] = jnp.zeros((stations, LANES), jnp.int32)
    meta[own, pl.ds(0, stations), pl.ds(0, windows)] = mask_ref[...]

    neighbours = (GROUP - 1) + has_before.astype(jnp.int32) + has_behind.astype(jnp.int32)
    pl.semaphore_wait(barrier, neighbours)

    def group_meta(step):
        return pltpu.make_async_remote_copy(
            src_ref=meta.at[own],
            dst_ref=meta.at[own],
            send_sem=meta_send.at[step - 1],
            recv_sem=meta_recv.at[step - 1],
            device_id={"sta": first + (rank + step) % GROUP},
            device_id_type=MESH,
        )

    def group_copy(index, step):
        peer = (rank + step) % GROUP
        start = pl.multiple_of(peer * share + index * chunk, LANES)
        return pltpu.make_async_remote_copy(
            src_ref=spec_ref.at[:, pl.ds(start, chunk)],
            dst_ref=held.at[index, own],
            send_sem=group_send.at[index, step - 1],
            recv_sem=group_recv.at[index, step - 1],
            device_id={"sta": first + peer},
            device_id_type=MESH,
        )

    def own_copy(index):
        start = pl.multiple_of(rank * share + index * chunk, LANES)
        return pltpu.make_async_copy(
            spec_ref.at[:, pl.ds(start, chunk)], held.at[index, own], local_sem.at[index]
        )

    def line_copy(index, down):
        source, target, peer = (GROUP, 0, behind) if down else (REACH, GROUP + REACH, before)
        return pltpu.make_async_remote_copy(
            src_ref=held.at[index, pl.ds(source, REACH)],
            dst_ref=held.at[index, pl.ds(target, REACH)],
            send_sem=line_send.at[index, int(down)],
            recv_sem=line_recv.at[index, int(down)],
            device_id={"sta": peer},
            device_id_type=MESH,
        )

    def meta_line(down):
        source, target, peer = (GROUP, 0, behind) if down else (REACH, GROUP + REACH, before)
        return pltpu.make_async_remote_copy(
            src_ref=meta.at[pl.ds(source, REACH)],
            dst_ref=meta.at[pl.ds(target, REACH)],
            send_sem=meta_line_send.at[int(down)],
            recv_sem=meta_line_recv.at[int(down)],
            device_id={"sta": peer},
            device_id_type=MESH,
        )

    steps = (2, 1, 3)
    for step in steps:
        group_meta(step).start()
    for index in range(CHUNKS):
        own_copy(index).start()
        for step in steps:
            group_copy(index, step).start()

    rank_cos = rank_table[0, pl.ds(rank, 1), :]
    rank_sin = rank_table[1, pl.ds(rank, 1), :]

    def fill(coarse, carry):
        step_cos = coarse_table[0, pl.ds(coarse, 1), :]
        step_sin = coarse_table[1, pl.ds(coarse, 1), :]
        base_cos = step_cos * rank_cos - step_sin * rank_sin
        base_sin = step_sin * rank_cos + step_cos * rank_sin
        index = (coarse * FINE) // chunk
        row = pl.multiple_of((coarse * FINE) % chunk, FINE)
        fine_cos = fine_table[0]
        fine_sin = fine_table[1]
        table[index, pl.ds(row, FINE), :] = (base_cos * fine_cos - base_sin * fine_sin).astype(
            jnp.bfloat16
        )
        table[index, pl.ds(chunk + row, FINE), :] = (
            -(base_sin * fine_cos + base_cos * fine_sin)
        ).astype(jnp.bfloat16)
        return carry

    lax.fori_loop(0, share // FINE, fill, 0)

    for step in steps:
        group_meta(step).wait_recv()
    slots_copy = pltpu.make_async_copy(
        meta.at[pl.ds(REACH, GROUP), pl.ds(stations, 8)], slot_smem, local_sem.at[CHUNKS]
    )
    slots_copy.start()

    @pl.when(has_behind)
    def _():
        meta_line(True).start()

    @pl.when(has_before)
    def _():
        meta_line(False).start()

    slots_copy.wait()

    def forward(index):
        own_copy(index).wait()
        for step in steps:
            group_copy(index, step).wait_recv()

        @pl.when(has_behind)
        def _():
            line_copy(index, True).start()

        @pl.when(has_before)
        def _():
            line_copy(index, False).start()

    def place(value):
        local = jnp.where(value < 0, REACH, value - (first - REACH))
        return jnp.clip(local, 0, held_blocks - 1)

    def work(index):
        @pl.when(has_before)
        def _():
            line_copy(index, True).wait_recv()

        @pl.when(has_behind)
        def _():
            line_copy(index, False).wait_recv()

        def widen(block, carry):
            start = pl.multiple_of(block * rows, rows)
            for tile in range(tiles):
                wide[tile, pl.ds(start, rows), :] = held[
                    index, block, :, pl.ds(tile * LANES, LANES)
                ].astype(jnp.float32)
            return carry

        lax.fori_loop(0, held_blocks, widen, 0)

        def slot_cross(place_at, carry):
            slot = place_at % slots
            owner = ((place_at // slots) % 2) * 2 + place_at // (2 * slots)
            left = place(slot_smem[owner, 0, slot * 2]) * rows
            right = place(slot_smem[owner, 0, slot * 2 + 1]) * rows
            out_row = pl.multiple_of(place_at * pairs, pairs)

            def tile_cross(tile, inner):
                column = pl.multiple_of(tile * LANES, LANES)
                right_real = [
                    wide[tile, pl.ds(right + 2 * w, stations, stride=per_station), :]
                    for w in range(windows)
                ]
                right_imag = [
                    wide[tile, pl.ds(right + 2 * w + 1, stations, stride=per_station), :]
                    for w in range(windows)
                ]
                for couple in range(0, stations, 2):
                    reals, imags = [], []
                    for station in (couple, couple + 1):
                        real = imag = None
                        for w in range(windows):
                            at = left + station * per_station + 2 * w
                            left_real = wide[tile, pl.ds(at, 1), :]
                            left_imag = wide[tile, pl.ds(at + 1, 1), :]
                            real_term = left_real * right_real[w] + left_imag * right_imag[w]
                            imag_term = left_imag * right_real[w] - left_real * right_imag[w]
                            real = real_term if real is None else real + real_term
                            imag = imag_term if imag is None else imag + imag_term
                        reals.append(real)
                        imags.append(imag)
                    at_row = out_row + couple * stations
                    cross[pl.ds(pl.multiple_of(at_row, 16), 16), pl.ds(column, LANES)] = (
                        jnp.concatenate(reals, axis=0).astype(jnp.bfloat16)
                    )
                    cross[
                        pl.ds(pl.multiple_of(at_row, 16), 16), pl.ds(chunk + column, LANES)
                    ] = jnp.concatenate(imags, axis=0).astype(jnp.bfloat16)
                return inner

            return lax.fori_loop(0, tiles, tile_cross, carry)

        lax.fori_loop(0, GROUP * slots, slot_cross, 0)

        half = 2 * slots * pairs
        width = 256

        def multiply(at, carry):
            column = pl.multiple_of(at * width, width)
            for k in range(2):
                product = jnp.dot(
                    cross[pl.ds(k * half, half), :],
                    table[index, :, pl.ds(column, width)],
                    preferred_element_type=jnp.float32,
                )
                if index > 0:
                    product = product + total[k, :, pl.ds(column, width)]
                total[k, :, pl.ds(column, width)] = product
            return carry

        lax.fori_loop(0, lags // width, multiply, 0)

    forward(0)
    for index in range(CHUNKS):
        if index + 1 < CHUNKS:
            forward(index + 1)
        work(index)

    mine = slots * pairs
    core_copy = pltpu.make_async_remote_copy(
        src_ref=total.at[1 - core],
        dst_ref=from_core,
        send_sem=sum_send.at[0],
        recv_sem=sum_recv.at[0],
        device_id={"sta": first + side * 2 + 1 - core},
        device_id_type=MESH,
    )
    core_copy.start()
    core_copy.wait_recv()
    other = pl.multiple_of((1 - side) * mine, mine)
    to_row[...] = (total[core, pl.ds(other, mine), :] + from_core[pl.ds(other, mine), :]).astype(
        jnp.bfloat16
    )
    row_copy = pltpu.make_async_remote_copy(
        src_ref=to_row,
        dst_ref=from_row,
        send_sem=sum_send.at[1],
        recv_sem=sum_recv.at[1],
        device_id={"sta": first + (rank + 2) % GROUP},
        device_id_type=MESH,
    )
    row_copy.start()

    @pl.when(has_before)
    def _():
        meta_line(True).wait_recv()

    @pl.when(has_behind)
    def _():
        meta_line(False).wait_recv()

    scales = []
    for slot in range(slots):
        left_mask = meta[place(pair_ref[slot, 0]), pl.ds(0, stations), :].astype(jnp.float32)
        right_mask = meta[place(pair_ref[slot, 1]), pl.ds(0, stations), :].astype(jnp.float32)
        counts = jnp.concatenate(
            [
                jnp.sum(left_mask[p : p + 1] * right_mask, axis=1, keepdims=True)
                for p in range(stations)
            ],
            axis=0,
        )
        live = jnp.where(pair_ref[slot, 0] >= 0, 1.0, 0.0)
        scales.append(live / (math.sqrt(freqs) * jnp.maximum(counts, 1.0)))

    row_copy.wait_recv()
    for slot in range(slots):
        start = pl.multiple_of(side * mine + slot * pairs, pairs)
        running = (
            total[core, pl.ds(start, pairs), :]
            + from_core[pl.ds(start, pairs), :]
            + from_row[pl.ds(slot * pairs, pairs), :].astype(jnp.float32)
        )
        out_ref[pl.ds(slot * pairs, pairs), :] = (running * scales[slot]).astype(jnp.bfloat16)

    core_copy.wait_send()
    row_copy.wait_send()
    for step in steps:
        group_meta(step).wait_send()
        for index in range(CHUNKS):
            group_copy(index, step).wait_send()

    @pl.when(has_behind)
    def _():
        meta_line(True).wait_send()
        for index in range(CHUNKS):
            line_copy(index, True).wait_send()

    @pl.when(has_before)
    def _():
        meta_line(False).wait_send()
        for index in range(CHUNKS):
            line_copy(index, False).wait_send()


def shards(groups, spectra, window_mask, pair_slots):
    stations, windows, _, freqs = spectra.shape
    slots = pair_slots.shape[0]
    rows = stations * windows * 2
    pairs = stations * stations
    held_blocks = GROUP + 2 * REACH
    share = freqs // GROUP
    chunk = share // CHUNKS
    masked = spectra * window_mask[:, :, None, None].astype(spectra.dtype)
    rank_table = phase_tables(np.arange(GROUP) * share, freqs, LAGS)
    coarse_table = phase_tables(np.arange(share // FINE) * FINE, freqs, LAGS)
    fine_table = phase_tables(np.arange(FINE), freqs, LAGS)
    vmem = pl.BlockSpec(memory_space=pltpu.VMEM)
    dma = pltpu.SemaphoreType.DMA
    dims = (stations, windows, slots, freqs, LAGS, groups)
    flops = 2 * GROUP * slots * pairs * 2 * share * LAGS
    out = pl.pallas_call(
        functools.partial(kernel, dims),
        out_shape=jax.ShapeDtypeStruct((slots * pairs, LAGS), jnp.bfloat16),
        in_specs=[vmem, vmem, pl.BlockSpec(memory_space=pltpu.SMEM), vmem, vmem, vmem],
        out_specs=vmem,
        scratch_shapes=[
            pltpu.VMEM((CHUNKS, held_blocks, rows, chunk), jnp.bfloat16),
            pltpu.VMEM((held_blocks, stations + 8, LANES), jnp.int32),
            pltpu.SMEM((GROUP, 8, LANES), jnp.int32),
            pltpu.VMEM((chunk // LANES, held_blocks * rows, LANES), jnp.float32),
            pltpu.VMEM((GROUP * slots * pairs, 2 * chunk), jnp.bfloat16),
            pltpu.VMEM((CHUNKS, 2 * chunk, LAGS), jnp.bfloat16),
            pltpu.VMEM((2, 2 * slots * pairs, LAGS), jnp.float32),
            pltpu.VMEM((2 * slots * pairs, LAGS), jnp.float32),
            pltpu.VMEM((slots * pairs, LAGS), jnp.bfloat16),
            pltpu.VMEM((slots * pairs, LAGS), jnp.bfloat16),
            dma((CHUNKS + 1,)),
            dma((CHUNKS, GROUP - 1)),
            dma((CHUNKS, GROUP - 1)),
            dma((CHUNKS, 2)),
            dma((CHUNKS, 2)),
            dma((GROUP - 1,)),
            dma((GROUP - 1,)),
            dma((2,)),
            dma((2,)),
            dma((2,)),
            dma((2,)),
        ],
        compiler_params=pltpu.CompilerParams(
            collective_id=0, has_side_effects=True, vmem_limit_bytes=48 * 1024 * 1024
        ),
        cost_estimate=pl.CostEstimate(flops=flops, bytes_accessed=4 * 2**20, transcendentals=0),
    )(
        masked.reshape(rows, freqs),
        window_mask,
        pair_slots,
        jnp.asarray(rank_table),
        jnp.asarray(coarse_table),
        jnp.asarray(fine_table),
    )
    return out.reshape(slots, stations, stations, LAGS)


def solution(mesh):
    placed = (P(("day", "sta"), None, None, None), P(("day", "sta"), None), P("sta", None))
    groups = mesh.shape["sta"] // GROUP
    return jax.shard_map(
        functools.partial(shards, groups),
        mesh=mesh,
        in_specs=placed,
        out_specs=P(("day", "sta"), None, None, None),
        check_vma=False,
    )
```

```python
import functools
import math

import jax
import jax.numpy as jnp
import numpy as np
from jax import lax
from jax.experimental import pallas as pl
from jax.experimental.pallas import tpu as pltpu
from jax.sharding import PartitionSpec as P

LAGS = 1024
REACH = 2
GROUP = 4
CHUNKS = 4
LANES = 128
FINE = 32
MESH = pl.DeviceIdType.MESH


def phase_tables(steps, frequency_values, lag_count):
    lag = np.arange(lag_count, dtype=np.int64) - lag_count // 2
    phase = np.mod(np.asarray(steps, np.int64)[:, None] * lag[None, :], 2 * frequency_values)
    angle = phase.astype(np.float64) * (math.pi / frequency_values)
    return np.stack([np.cos(angle), np.sin(angle)]).astype(np.float32)


def kernel(
    dims,
    raw_ref,
    mask_ref,
    pair_ref,
    rank_table,
    coarse_table,
    fine_table,
    out_ref,
    spec_ref,
    mask_rows,
    held,
    meta,
    slot_smem,
    wide,
    cross_even,
    cross_odd,
    table,
    total,
    from_core,
    to_row,
    from_row,
    local_sem,
    group_send,
    group_recv,
    line_send,
    line_recv,
    meta_send,
    meta_recv,
    meta_line_send,
    meta_line_recv,
    core_send,
    core_recv,
    row_send,
    row_recv,
):
    stations, windows, slots, freqs, lags, groups = dims
    rows = stations * windows * 2
    per_station = windows * 2
    pairs = stations * stations
    held_blocks = GROUP + 2 * REACH
    share = freqs // GROUP
    chunk = share // CHUNKS
    tiles = chunk // LANES

    me = lax.axis_index("sta")
    group = me // GROUP
    rank = me % GROUP
    core = rank % 2
    side = rank // 2
    first = group * GROUP
    has_before = group > 0
    has_behind = group < groups - 1
    before = me - GROUP
    behind = me + GROUP

    barrier = pltpu.get_barrier_semaphore()
    for step in range(1, GROUP):
        pl.semaphore_signal(
            barrier, inc=1, device_id={"sta": first + (rank + step) % GROUP}, device_id_type=MESH
        )

    @pl.when(has_before)
    def _():
        pl.semaphore_signal(barrier, inc=1, device_id={"sta": before}, device_id_type=MESH)

    @pl.when(has_behind)
    def _():
        pl.semaphore_signal(barrier, inc=1, device_id={"sta": behind}, device_id_type=MESH)

    own = REACH + rank
    lane = lax.broadcasted_iota(jnp.int32, (8, LANES), 1)
    slot_row = jnp.zeros((8, LANES), jnp.int32)
    for slot in range(slots):
        for end in range(2):
            slot_row = jnp.where(lane == slot * 2 + end, pair_ref[slot, end], slot_row)
    meta[own, pl.ds(stations, 8), :] = slot_row
    meta[own, pl.ds(0, stations), :] = jnp.zeros((stations, LANES), jnp.int32)
    meta[own, pl.ds(0, stations), pl.ds(0, windows)] = mask_ref[...]

    for w in range(windows):
        valid = jnp.broadcast_to(
            mask_ref[:, pl.ds(w, 1)].astype(jnp.float32), (stations, LANES)
        )
        for part in range(2):
            mask_rows[pl.ds(2 * w + part, stations, stride=per_station), :] = valid

    def mask_tile(tile, carry):
        column = pl.ds(pl.multiple_of(tile * LANES, LANES), LANES)
        spec_ref[:, column] = raw_ref[:, column] * mask_rows[...].astype(jnp.bfloat16)
        return carry

    lax.fori_loop(0, freqs // LANES, mask_tile, 0, unroll=4)

    neighbours = (GROUP - 1) + has_before.astype(jnp.int32) + has_behind.astype(jnp.int32)
    pl.semaphore_wait(barrier, neighbours)

    def group_meta(step):
        return pltpu.make_async_remote_copy(
            src_ref=meta.at[own],
            dst_ref=meta.at[own],
            send_sem=meta_send.at[step - 1],
            recv_sem=meta_recv.at[step - 1],
            device_id={"sta": first + (rank + step) % GROUP},
            device_id_type=MESH,
        )

    def group_copy(index, step):
        peer = (rank + step) % GROUP
        start = pl.multiple_of(peer * share + index * chunk, LANES)
        return pltpu.make_async_remote_copy(
            src_ref=spec_ref.at[:, pl.ds(start, chunk)],
            dst_ref=held.at[index, own],
            send_sem=group_send.at[index, step - 1],
            recv_sem=group_recv.at[index, step - 1],
            device_id={"sta": first + peer},
            device_id_type=MESH,
        )

    def own_copy(index):
        start = pl.multiple_of(rank * share + index * chunk, LANES)
        return pltpu.make_async_copy(
            spec_ref.at[:, pl.ds(start, chunk)], held.at[index, own], local_sem.at[index]
        )

    def line_copy(index, down):
        source, target, peer = (GROUP, 0, behind) if down else (REACH, GROUP + REACH, before)
        return pltpu.make_async_remote_copy(
            src_ref=held.at[index, pl.ds(source, REACH)],
            dst_ref=held.at[index, pl.ds(target, REACH)],
            send_sem=line_send.at[index, int(down)],
            recv_sem=line_recv.at[index, int(down)],
            device_id={"sta": peer},
            device_id_type=MESH,
        )

    def meta_line(down):
        source, target, peer = (GROUP, 0, behind) if down else (REACH, GROUP + REACH, before)
        return pltpu.make_async_remote_copy(
            src_ref=meta.at[pl.ds(source, REACH)],
            dst_ref=meta.at[pl.ds(target, REACH)],
            send_sem=meta_line_send.at[int(down)],
            recv_sem=meta_line_recv.at[int(down)],
            device_id={"sta": peer},
            device_id_type=MESH,
        )

    steps = (2, 1, 3)
    for step in steps:
        group_meta(step).start()
    for index in range(CHUNKS):
        own_copy(index).start()
        for step in steps:
            group_copy(index, step).start()

    rank_cos = rank_table[0, pl.ds(rank, 1), :]
    rank_sin = rank_table[1, pl.ds(rank, 1), :]

    def fill(coarse, carry):
        step_cos = coarse_table[0, pl.ds(coarse, 1), :]
        step_sin = coarse_table[1, pl.ds(coarse, 1), :]
        base_cos = step_cos * rank_cos - step_sin * rank_sin
        base_sin = step_sin * rank_cos + step_cos * rank_sin
        index = (coarse * FINE) // chunk
        row = pl.multiple_of((coarse * FINE) % chunk, FINE)
        fine_cos = fine_table[0]
        fine_sin = fine_table[1]
        table[index, pl.ds(row, FINE), :] = (base_cos * fine_cos - base_sin * fine_sin).astype(
            jnp.bfloat16
        )
        table[index, pl.ds(chunk + row, FINE), :] = (
            -(base_sin * fine_cos + base_cos * fine_sin)
        ).astype(jnp.bfloat16)
        return carry

    lax.fori_loop(0, share // FINE, fill, 0)

    for step in steps:
        group_meta(step).wait_recv()
    slots_copy = pltpu.make_async_copy(
        meta.at[pl.ds(REACH, GROUP), pl.ds(stations, 8)], slot_smem, local_sem.at[CHUNKS]
    )
    slots_copy.start()

    @pl.when(has_behind)
    def _():
        meta_line(True).start()

    @pl.when(has_before)
    def _():
        meta_line(False).start()

    slots_copy.wait()

    def forward(index):
        own_copy(index).wait()
        for step in steps:
            group_copy(index, step).wait_recv()

        @pl.when(has_behind)
        def _():
            line_copy(index, True).start()

        @pl.when(has_before)
        def _():
            line_copy(index, False).start()

    def place(value):
        local = jnp.where(value < 0, REACH, value - (first - REACH))
        return jnp.clip(local, 0, held_blocks - 1)

    half = 2 * slots * pairs
    width = lags // (2 * slots)
    cross_of = (cross_even, cross_odd)

    def product(index, k, column):
        part = jnp.dot(
            cross_of[index % 2][pl.ds(pl.multiple_of(k * half, half), half), :],
            table[index, :, pl.ds(column, width)],
            preferred_element_type=jnp.float32,
        )
        if index > 0:
            part = part + total[k, :, pl.ds(column, width)]
        total[k, :, pl.ds(column, width)] = part

    def work(index):
        @pl.when(has_before)
        def _():
            line_copy(index, True).wait_recv()

        @pl.when(has_behind)
        def _():
            line_copy(index, False).wait_recv()

        def widen(block, carry):
            for tile in range(tiles):
                wide[tile, block] = held[
                    index, block, :, pl.ds(tile * LANES, LANES)
                ].astype(jnp.float32)
            return carry

        lax.fori_loop(0, held_blocks, widen, 0)
        cross = cross_of[index % 2]

        def slot_cross(place_at, carry):
            if index > 0:
                product(
                    index - 1, place_at % 2, pl.multiple_of((place_at // 2) * width, width)
                )
            slot = place_at % slots
            owner = ((place_at // slots) % 2) * 2 + place_at // (2 * slots)
            left = place(slot_smem[owner, 0, slot * 2])
            right = place(slot_smem[owner, 0, slot * 2 + 1])
            out_row = pl.multiple_of(place_at * pairs, pairs)
            for tile in range(tiles):
                column = tile * LANES
                right_real = [
                    wide[tile, right, pl.ds(2 * w, stations, stride=per_station), :]
                    for w in range(windows)
                ]
                right_imag = [
                    wide[tile, right, pl.ds(2 * w + 1, stations, stride=per_station), :]
                    for w in range(windows)
                ]
                for couple in range(0, stations, 2):
                    reals, imags = [], []
                    for station in (couple, couple + 1):
                        real = imag = None
                        for w in range(windows):
                            at = station * per_station + 2 * w
                            left_real = wide[tile, left, pl.ds(at, 1), :]
                            left_imag = wide[tile, left, pl.ds(at + 1, 1), :]
                            real_term = left_real * right_real[w] + left_imag * right_imag[w]
                            imag_term = left_imag * right_real[w] - left_real * right_imag[w]
                            real = real_term if real is None else real + real_term
                            imag = imag_term if imag is None else imag + imag_term
                        reals.append(real)
                        imags.append(imag)
                    at_row = pl.ds(pl.multiple_of(out_row + couple * stations, 16), 16)
                    cross[at_row, pl.ds(column, LANES)] = jnp.concatenate(reals, axis=0).astype(
                        jnp.bfloat16
                    )
                    cross[at_row, pl.ds(chunk + column, LANES)] = jnp.concatenate(
                        imags, axis=0
                    ).astype(jnp.bfloat16)
            return carry

        lax.fori_loop(0, GROUP * slots, slot_cross, 0)

    forward(0)
    for index in range(CHUNKS):
        if index + 1 < CHUNKS:
            forward(index + 1)
        work(index)

    mine = slots * pairs
    pieces = lags // width

    def core_copy(piece):
        column = pl.ds(pl.multiple_of(piece * width, width), width)
        return pltpu.make_async_remote_copy(
            src_ref=total.at[1 - core, :, column],
            dst_ref=from_core.at[:, column],
            send_sem=core_send.at[piece],
            recv_sem=core_recv.at[piece],
            device_id={"sta": first + side * 2 + 1 - core},
            device_id_type=MESH,
        )

    def row_copy(piece):
        column = pl.ds(pl.multiple_of(piece * width, width), width)
        return pltpu.make_async_remote_copy(
            src_ref=to_row.at[:, column],
            dst_ref=from_row.at[:, column],
            send_sem=row_send.at[piece],
            recv_sem=row_recv.at[piece],
            device_id={"sta": first + (rank + 2) % GROUP},
            device_id_type=MESH,
        )

    def last_of_partner(piece, carry):
        product(CHUNKS - 1, 1 - core, pl.multiple_of(piece * width, width))
        core_copy(piece).start()
        return carry

    lax.fori_loop(0, pieces, last_of_partner, 0)
    other = pl.multiple_of((1 - side) * mine, mine)

    def last_of_own(piece, carry):
        column = pl.ds(pl.multiple_of(piece * width, width), width)
        product(CHUNKS - 1, core, pl.multiple_of(piece * width, width))
        core_copy(piece).wait_recv()
        to_row[:, column] = (
            total[core, pl.ds(other, mine), column] + from_core[pl.ds(other, mine), column]
        ).astype(jnp.bfloat16)
        row_copy(piece).start()
        return carry

    lax.fori_loop(0, pieces, last_of_own, 0)

    @pl.when(has_before)
    def _():
        meta_line(True).wait_recv()

    @pl.when(has_behind)
    def _():
        meta_line(False).wait_recv()

    scales = []
    for slot in range(slots):
        left_mask = meta[place(pair_ref[slot, 0]), pl.ds(0, stations), :].astype(jnp.float32)
        right_mask = meta[place(pair_ref[slot, 1]), pl.ds(0, stations), :].astype(jnp.float32)
        counts = jnp.concatenate(
            [
                jnp.sum(left_mask[p : p + 1] * right_mask, axis=1, keepdims=True)
                for p in range(stations)
            ],
            axis=0,
        )
        live = jnp.where(pair_ref[slot, 0] >= 0, 1.0, 0.0)
        scales.append(live / (math.sqrt(freqs) * jnp.maximum(counts, 1.0)))

    def finish(piece, carry):
        column = pl.ds(pl.multiple_of(piece * width, width), width)
        row_copy(piece).wait_recv()
        for slot in range(slots):
            start = pl.multiple_of(side * mine + slot * pairs, pairs)
            running = (
                total[core, pl.ds(start, pairs), column]
                + from_core[pl.ds(start, pairs), column]
                + from_row[pl.ds(slot * pairs, pairs), column].astype(jnp.float32)
            )
            out_ref[pl.ds(slot * pairs, pairs), column] = (running * scales[slot]).astype(
                jnp.bfloat16
            )
        return carry

    lax.fori_loop(0, pieces, finish, 0)

    for piece in range(pieces):
        core_copy(piece).wait_send()
        row_copy(piece).wait_send()
    for step in steps:
        group_meta(step).wait_send()
        for index in range(CHUNKS):
            group_copy(index, step).wait_send()

    @pl.when(has_behind)
    def _():
        meta_line(True).wait_send()
        for index in range(CHUNKS):
            line_copy(index, True).wait_send()

    @pl.when(has_before)
    def _():
        meta_line(False).wait_send()
        for index in range(CHUNKS):
            line_copy(index, False).wait_send()


def shards(groups, spectra, window_mask, pair_slots):
    stations, windows, _, freqs = spectra.shape
    slots = pair_slots.shape[0]
    rows = stations * windows * 2
    pairs = stations * stations
    held_blocks = GROUP + 2 * REACH
    share = freqs // GROUP
    chunk = share // CHUNKS
    rank_table = phase_tables(np.arange(GROUP) * share, freqs, LAGS)
    coarse_table = phase_tables(np.arange(share // FINE) * FINE, freqs, LAGS)
    fine_table = phase_tables(np.arange(FINE), freqs, LAGS)
    vmem = pl.BlockSpec(memory_space=pltpu.VMEM)
    dma = pltpu.SemaphoreType.DMA
    dims = (stations, windows, slots, freqs, LAGS, groups)
    flops = 2 * GROUP * slots * pairs * 2 * share * LAGS
    out = pl.pallas_call(
        functools.partial(kernel, dims),
        out_shape=jax.ShapeDtypeStruct((slots * pairs, LAGS), jnp.bfloat16),
        in_specs=[vmem, vmem, pl.BlockSpec(memory_space=pltpu.SMEM), vmem, vmem, vmem],
        out_specs=vmem,
        scratch_shapes=[
            pltpu.VMEM((rows, freqs), jnp.bfloat16),
            pltpu.VMEM((rows, LANES), jnp.float32),
            pltpu.VMEM((CHUNKS, held_blocks, rows, chunk), jnp.bfloat16),
            pltpu.VMEM((held_blocks, stations + 8, LANES), jnp.int32),
            pltpu.SMEM((GROUP, 8, LANES), jnp.int32),
            pltpu.VMEM((chunk // LANES, held_blocks, rows, LANES), jnp.float32),
            pltpu.VMEM((GROUP * slots * pairs, 2 * chunk), jnp.bfloat16),
            pltpu.VMEM((GROUP * slots * pairs, 2 * chunk), jnp.bfloat16),
            pltpu.VMEM((CHUNKS, 2 * chunk, LAGS), jnp.bfloat16),
            pltpu.VMEM((2, 2 * slots * pairs, LAGS), jnp.float32),
            pltpu.VMEM((2 * slots * pairs, LAGS), jnp.float32),
            pltpu.VMEM((slots * pairs, LAGS), jnp.bfloat16),
            pltpu.VMEM((slots * pairs, LAGS), jnp.bfloat16),
            dma((CHUNKS + 1,)),
            dma((CHUNKS, GROUP - 1)),
            dma((CHUNKS, GROUP - 1)),
            dma((CHUNKS, 2)),
            dma((CHUNKS, 2)),
            dma((GROUP - 1,)),
            dma((GROUP - 1,)),
            dma((2,)),
            dma((2,)),
            dma((2 * slots,)),
            dma((2 * slots,)),
            dma((2 * slots,)),
            dma((2 * slots,)),
        ],
        compiler_params=pltpu.CompilerParams(
            collective_id=0, has_side_effects=True, vmem_limit_bytes=48 * 1024 * 1024
        ),
        cost_estimate=pl.CostEstimate(flops=flops, bytes_accessed=4 * 2**20, transcendentals=0),
    )(
        spectra.reshape(rows, freqs),
        window_mask,
        pair_slots,
        jnp.asarray(rank_table),
        jnp.asarray(coarse_table),
        jnp.asarray(fine_table),
    )
    return out.reshape(slots, stations, stations, LAGS)


def solution(mesh):
    placed = (P(("day", "sta"), None, None, None), P(("day", "sta"), None), P("sta", None))
    groups = mesh.shape["sta"] // GROUP
    return jax.shard_map(
        functools.partial(shards, groups),
        mesh=mesh,
        in_specs=placed,
        out_specs=P(("day", "sta"), None, None, None),
        check_vma=False,
    )
```

```python
import functools
import math

import jax
import jax.numpy as jnp
import numpy as np
from jax import lax
from jax.experimental import pallas as pl
from jax.experimental.pallas import tpu as pltpu
from jax.sharding import PartitionSpec as P

LAGS = 1024
REACH = 2
GROUP = 4
CHUNKS = 8
LANES = 128
FINE = 32
MESH = pl.DeviceIdType.MESH


def phase_tables(steps, frequency_values, lag_count):
    lag = np.arange(lag_count, dtype=np.int64) - lag_count // 2
    phase = np.mod(np.asarray(steps, np.int64)[:, None] * lag[None, :], 2 * frequency_values)
    angle = phase.astype(np.float64) * (math.pi / frequency_values)
    return np.stack([np.cos(angle), np.sin(angle)]).astype(np.float32)


def kernel(
    dims,
    raw_ref,
    mask_ref,
    pair_ref,
    rank_table,
    coarse_table,
    fine_table,
    out_ref,
    spec_ref,
    mask_rows,
    held,
    meta,
    slot_smem,
    wide,
    cross_even,
    cross_odd,
    table,
    total,
    from_core,
    to_row,
    from_row,
    local_sem,
    group_send,
    group_recv,
    line_send,
    line_recv,
    meta_send,
    meta_recv,
    meta_line_send,
    meta_line_recv,
    core_send,
    core_recv,
    row_send,
    row_recv,
):
    stations, windows, slots, freqs, lags, groups = dims
    rows = stations * windows * 2
    per_station = windows * 2
    pairs = stations * stations
    held_blocks = GROUP + 2 * REACH
    share = freqs // GROUP
    chunk = share // CHUNKS
    tiles = chunk // LANES

    me = lax.axis_index("sta")
    group = me // GROUP
    rank = me % GROUP
    core = rank % 2
    side = rank // 2
    first = group * GROUP
    has_before = group > 0
    has_behind = group < groups - 1
    before = me - GROUP
    behind = me + GROUP

    barrier = pltpu.get_barrier_semaphore()
    for step in range(1, GROUP):
        pl.semaphore_signal(
            barrier, inc=1, device_id={"sta": first + (rank + step) % GROUP}, device_id_type=MESH
        )

    @pl.when(has_before)
    def _():
        pl.semaphore_signal(barrier, inc=1, device_id={"sta": before}, device_id_type=MESH)

    @pl.when(has_behind)
    def _():
        pl.semaphore_signal(barrier, inc=1, device_id={"sta": behind}, device_id_type=MESH)

    own = REACH + rank
    lane = lax.broadcasted_iota(jnp.int32, (8, LANES), 1)
    slot_row = jnp.zeros((8, LANES), jnp.int32)
    for slot in range(slots):
        for end in range(2):
            slot_row = jnp.where(lane == slot * 2 + end, pair_ref[slot, end], slot_row)
    meta[own, pl.ds(stations, 8), :] = slot_row
    meta[own, pl.ds(0, stations), :] = jnp.zeros((stations, LANES), jnp.int32)
    meta[own, pl.ds(0, stations), pl.ds(0, windows)] = mask_ref[...]

    for w in range(windows):
        valid = jnp.broadcast_to(
            mask_ref[:, pl.ds(w, 1)].astype(jnp.float32), (stations, LANES)
        )
        for part in range(2):
            mask_rows[pl.ds(2 * w + part, stations, stride=per_station), :] = valid

    def mask_part(part, carry):
        valid = mask_rows[...].astype(jnp.bfloat16)
        for tile in range(tiles):
            column = pl.multiple_of(part * chunk + tile * LANES, LANES)
            spec_ref[part, :, pl.ds(tile * LANES, LANES)] = raw_ref[:, pl.ds(column, LANES)] * valid
        return carry

    lax.fori_loop(0, GROUP * CHUNKS, mask_part, 0, unroll=2)

    neighbours = (GROUP - 1) + has_before.astype(jnp.int32) + has_behind.astype(jnp.int32)
    pl.semaphore_wait(barrier, neighbours)

    def group_meta(step):
        return pltpu.make_async_remote_copy(
            src_ref=meta.at[own],
            dst_ref=meta.at[own],
            send_sem=meta_send.at[step - 1],
            recv_sem=meta_recv.at[step - 1],
            device_id={"sta": first + (rank + step) % GROUP},
            device_id_type=MESH,
        )

    def group_copy(index, step):
        peer = (rank + step) % GROUP
        return pltpu.make_async_remote_copy(
            src_ref=spec_ref.at[peer * CHUNKS + index],
            dst_ref=held.at[index, own],
            send_sem=group_send.at[index, step - 1],
            recv_sem=group_recv.at[index, step - 1],
            device_id={"sta": first + peer},
            device_id_type=MESH,
        )

    def own_copy(index):
        return pltpu.make_async_copy(
            spec_ref.at[rank * CHUNKS + index], held.at[index, own], local_sem.at[index]
        )

    def line_copy(index, down):
        source, target, peer = (GROUP, 0, behind) if down else (REACH, GROUP + REACH, before)
        return pltpu.make_async_remote_copy(
            src_ref=held.at[index, pl.ds(source, REACH)],
            dst_ref=held.at[index, pl.ds(target, REACH)],
            send_sem=line_send.at[index, int(down)],
            recv_sem=line_recv.at[index, int(down)],
            device_id={"sta": peer},
            device_id_type=MESH,
        )

    def meta_line(down):
        source, target, peer = (GROUP, 0, behind) if down else (REACH, GROUP + REACH, before)
        return pltpu.make_async_remote_copy(
            src_ref=meta.at[pl.ds(source, REACH)],
            dst_ref=meta.at[pl.ds(target, REACH)],
            send_sem=meta_line_send.at[int(down)],
            recv_sem=meta_line_recv.at[int(down)],
            device_id={"sta": peer},
            device_id_type=MESH,
        )

    steps = (2, 1, 3)
    for step in steps:
        group_meta(step).start()
    for index in range(CHUNKS):
        own_copy(index).start()
        for step in steps:
            group_copy(index, step).start()

    rank_cos = rank_table[0, pl.ds(rank, 1), :]
    rank_sin = rank_table[1, pl.ds(rank, 1), :]

    def fill(index, step, carry):
        coarse = index * (chunk // FINE) + step
        step_cos = coarse_table[0, pl.ds(coarse, 1), :]
        step_sin = coarse_table[1, pl.ds(coarse, 1), :]
        base_cos = step_cos * rank_cos - step_sin * rank_sin
        base_sin = step_sin * rank_cos + step_cos * rank_sin
        row = pl.multiple_of(step * FINE, FINE)
        fine_cos = fine_table[0]
        fine_sin = fine_table[1]
        table[index, pl.ds(row, FINE), :] = (base_cos * fine_cos - base_sin * fine_sin).astype(
            jnp.bfloat16
        )
        table[index, pl.ds(chunk + row, FINE), :] = (
            -(base_sin * fine_cos + base_cos * fine_sin)
        ).astype(jnp.bfloat16)
        return carry

    def forward(index):
        own_copy(index).wait()
        for step in steps:
            group_copy(index, step).wait_recv()

        @pl.when(has_behind)
        def _():
            line_copy(index, True).start()

        @pl.when(has_before)
        def _():
            line_copy(index, False).start()

    def place(value):
        local = jnp.where(value < 0, REACH, value - (first - REACH))
        return jnp.clip(local, 0, held_blocks - 1)

    half = 2 * slots * pairs
    width = lags // (2 * slots)
    cross_of = (cross_even, cross_odd)

    def product(index, k, column):
        part = jnp.dot(
            cross_of[index % 2][pl.ds(pl.multiple_of(k * half, half), half), :],
            table[index, :, pl.ds(column, width)],
            preferred_element_type=jnp.float32,
        )
        if index > 0:
            part = part + total[k, :, pl.ds(column, width)]
        total[k, :, pl.ds(column, width)] = part

    def work(index):
        @pl.when(has_before)
        def _():
            line_copy(index, True).wait_recv()

        @pl.when(has_behind)
        def _():
            line_copy(index, False).wait_recv()

        def widen(block, carry):
            for tile in range(tiles):
                wide[tile, block] = held[
                    index, block, :, pl.ds(tile * LANES, LANES)
                ].astype(jnp.float32)
            return carry

        lax.fori_loop(0, held_blocks, widen, 0)
        cross = cross_of[index % 2]

        def slot_cross(place_at, carry):
            if index > 0:
                product(
                    index - 1, place_at % 2, pl.multiple_of((place_at // 2) * width, width)
                )
            slot = place_at % slots
            owner = ((place_at // slots) % 2) * 2 + place_at // (2 * slots)
            left = place(slot_smem[owner, 0, slot * 2])
            right = place(slot_smem[owner, 0, slot * 2 + 1])
            out_row = pl.multiple_of(place_at * pairs, pairs)
            for tile in range(tiles):
                column = tile * LANES
                right_real = [
                    wide[tile, right, pl.ds(2 * w, stations, stride=per_station), :]
                    for w in range(windows)
                ]
                right_imag = [
                    wide[tile, right, pl.ds(2 * w + 1, stations, stride=per_station), :]
                    for w in range(windows)
                ]
                for couple in range(0, stations, 2):
                    reals, imags = [], []
                    for station in (couple, couple + 1):
                        real = imag = None
                        for w in range(windows):
                            at = station * per_station + 2 * w
                            left_real = wide[tile, left, pl.ds(at, 1), :]
                            left_imag = wide[tile, left, pl.ds(at + 1, 1), :]
                            real_term = left_real * right_real[w] + left_imag * right_imag[w]
                            imag_term = left_imag * right_real[w] - left_real * right_imag[w]
                            real = real_term if real is None else real + real_term
                            imag = imag_term if imag is None else imag + imag_term
                        reals.append(real)
                        imags.append(imag)
                    at_row = pl.ds(pl.multiple_of(out_row + couple * stations, 16), 16)
                    cross[at_row, pl.ds(column, LANES)] = jnp.concatenate(reals, axis=0).astype(
                        jnp.bfloat16
                    )
                    cross[at_row, pl.ds(chunk + column, LANES)] = jnp.concatenate(
                        imags, axis=0
                    ).astype(jnp.bfloat16)
            return carry

        lax.fori_loop(0, GROUP * slots, slot_cross, 0)

    forward(0)
    for step in steps:
        group_meta(step).wait_recv()
    slots_copy = pltpu.make_async_copy(
        meta.at[pl.ds(REACH, GROUP), pl.ds(stations, 8)], slot_smem, local_sem.at[CHUNKS]
    )
    slots_copy.start()

    @pl.when(has_behind)
    def _():
        meta_line(True).start()

    @pl.when(has_before)
    def _():
        meta_line(False).start()

    slots_copy.wait()

    for index in range(CHUNKS):
        if index + 1 < CHUNKS:
            forward(index + 1)
        lax.fori_loop(0, chunk // FINE, functools.partial(fill, index), 0)
        work(index)

    mine = slots * pairs
    pieces = lags // width

    def core_copy(piece, to_side):
        column = pl.ds(pl.multiple_of(piece * width, width), width)
        start = pl.multiple_of(to_side * mine, mine)
        return pltpu.make_async_remote_copy(
            src_ref=total.at[1 - core, pl.ds(start, mine), column],
            dst_ref=from_core.at[pl.ds(start, mine), column],
            send_sem=core_send.at[to_side, piece],
            recv_sem=core_recv.at[to_side, piece],
            device_id={"sta": first + side * 2 + 1 - core},
            device_id_type=MESH,
        )

    def row_copy(piece):
        return pltpu.make_async_remote_copy(
            src_ref=to_row.at[piece],
            dst_ref=from_row.at[piece],
            send_sem=row_send.at[piece],
            recv_sem=row_recv.at[piece],
            device_id={"sta": first + (rank + 2) % GROUP},
            device_id_type=MESH,
        )

    def last_of_partner(piece, carry):
        product(CHUNKS - 1, 1 - core, pl.multiple_of(piece * width, width))
        core_copy(piece, 1 - side).start()
        return carry

    lax.fori_loop(0, pieces, last_of_partner, 0)
    for piece in range(pieces):
        core_copy(piece, side).start()
    other = pl.multiple_of((1 - side) * mine, mine)

    def last_of_own(piece, carry):
        column = pl.ds(pl.multiple_of(piece * width, width), width)
        product(CHUNKS - 1, core, pl.multiple_of(piece * width, width))
        core_copy(piece, 1 - side).wait_recv()
        to_row[piece] = (
            total[core, pl.ds(other, mine), column] + from_core[pl.ds(other, mine), column]
        ).astype(jnp.bfloat16)
        row_copy(piece).start()
        return carry

    lax.fori_loop(0, pieces, last_of_own, 0)

    @pl.when(has_before)
    def _():
        meta_line(True).wait_recv()

    @pl.when(has_behind)
    def _():
        meta_line(False).wait_recv()

    scales = []
    for slot in range(slots):
        left_mask = meta[place(pair_ref[slot, 0]), pl.ds(0, stations), :].astype(jnp.float32)
        right_mask = meta[place(pair_ref[slot, 1]), pl.ds(0, stations), :].astype(jnp.float32)
        counts = jnp.concatenate(
            [
                jnp.sum(left_mask[p : p + 1] * right_mask, axis=1, keepdims=True)
                for p in range(stations)
            ],
            axis=0,
        )
        live = jnp.where(pair_ref[slot, 0] >= 0, 1.0, 0.0)
        scales.append(live / (math.sqrt(freqs) * jnp.maximum(counts, 1.0)))

    def finish(piece, carry):
        column = pl.ds(pl.multiple_of(piece * width, width), width)
        core_copy(piece, side).wait_recv()
        row_copy(piece).wait_recv()
        for slot in range(slots):
            start = pl.multiple_of(side * mine + slot * pairs, pairs)
            running = (
                total[core, pl.ds(start, pairs), column]
                + from_core[pl.ds(start, pairs), column]
                + from_row[piece, pl.ds(slot * pairs, pairs), :].astype(jnp.float32)
            )
            out_ref[pl.ds(slot * pairs, pairs), column] = (running * scales[slot]).astype(
                jnp.bfloat16
            )
        return carry

    lax.fori_loop(0, pieces, finish, 0)

    for piece in range(pieces):
        core_copy(piece, side).wait_send()
        core_copy(piece, 1 - side).wait_send()
        row_copy(piece).wait_send()
    for step in steps:
        group_meta(step).wait_send()
        for index in range(CHUNKS):
            group_copy(index, step).wait_send()

    @pl.when(has_behind)
    def _():
        meta_line(True).wait_send()
        for index in range(CHUNKS):
            line_copy(index, True).wait_send()

    @pl.when(has_before)
    def _():
        meta_line(False).wait_send()
        for index in range(CHUNKS):
            line_copy(index, False).wait_send()


def shards(groups, spectra, window_mask, pair_slots):
    stations, windows, _, freqs = spectra.shape
    slots = pair_slots.shape[0]
    rows = stations * windows * 2
    pairs = stations * stations
    held_blocks = GROUP + 2 * REACH
    share = freqs // GROUP
    chunk = share // CHUNKS
    rank_table = phase_tables(np.arange(GROUP) * share, freqs, LAGS)
    coarse_table = phase_tables(np.arange(share // FINE) * FINE, freqs, LAGS)
    fine_table = phase_tables(np.arange(FINE), freqs, LAGS)
    vmem = pl.BlockSpec(memory_space=pltpu.VMEM)
    dma = pltpu.SemaphoreType.DMA
    dims = (stations, windows, slots, freqs, LAGS, groups)
    flops = 2 * GROUP * slots * pairs * 2 * share * LAGS
    out = pl.pallas_call(
        functools.partial(kernel, dims),
        out_shape=jax.ShapeDtypeStruct((slots * pairs, LAGS), jnp.bfloat16),
        in_specs=[vmem, vmem, pl.BlockSpec(memory_space=pltpu.SMEM), vmem, vmem, vmem],
        out_specs=vmem,
        scratch_shapes=[
            pltpu.VMEM((GROUP * CHUNKS, rows, chunk), jnp.bfloat16),
            pltpu.VMEM((rows, LANES), jnp.float32),
            pltpu.VMEM((CHUNKS, held_blocks, rows, chunk), jnp.bfloat16),
            pltpu.VMEM((held_blocks, stations + 8, LANES), jnp.int32),
            pltpu.SMEM((GROUP, 8, LANES), jnp.int32),
            pltpu.VMEM((chunk // LANES, held_blocks, rows, LANES), jnp.float32),
            pltpu.VMEM((GROUP * slots * pairs, 2 * chunk), jnp.bfloat16),
            pltpu.VMEM((GROUP * slots * pairs, 2 * chunk), jnp.bfloat16),
            pltpu.VMEM((CHUNKS, 2 * chunk, LAGS), jnp.bfloat16),
            pltpu.VMEM((2, 2 * slots * pairs, LAGS), jnp.float32),
            pltpu.VMEM((2 * slots * pairs, LAGS), jnp.float32),
            pltpu.VMEM((2 * slots, slots * pairs, LAGS // (2 * slots)), jnp.bfloat16),
            pltpu.VMEM((2 * slots, slots * pairs, LAGS // (2 * slots)), jnp.bfloat16),
            dma((CHUNKS + 1,)),
            dma((CHUNKS, GROUP - 1)),
            dma((CHUNKS, GROUP - 1)),
            dma((CHUNKS, 2)),
            dma((CHUNKS, 2)),
            dma((GROUP - 1,)),
            dma((GROUP - 1,)),
            dma((2,)),
            dma((2,)),
            dma((2, 2 * slots)),
            dma((2, 2 * slots)),
            dma((2 * slots,)),
            dma((2 * slots,)),
        ],
        compiler_params=pltpu.CompilerParams(
            collective_id=0, has_side_effects=True, vmem_limit_bytes=48 * 1024 * 1024
        ),
        cost_estimate=pl.CostEstimate(flops=flops, bytes_accessed=4 * 2**20, transcendentals=0),
    )(
        spectra.reshape(rows, freqs),
        window_mask,
        pair_slots,
        jnp.asarray(rank_table),
        jnp.asarray(coarse_table),
        jnp.asarray(fine_table),
    )
    return out.reshape(slots, stations, stations, LAGS)


def solution(mesh):
    placed = (P(("day", "sta"), None, None, None), P(("day", "sta"), None), P("sta", None))
    groups = mesh.shape["sta"] // GROUP
    return jax.shard_map(
        functools.partial(shards, groups),
        mesh=mesh,
        in_specs=placed,
        out_specs=P(("day", "sta"), None, None, None),
        check_vma=False,
    )
```

```python
import functools
import math

import jax
import jax.numpy as jnp
import numpy as np
from jax import lax
from jax.experimental import pallas as pl
from jax.experimental.pallas import tpu as pltpu
from jax.sharding import PartitionSpec as P

LAGS = 1024
REACH = 2
GROUP = 4
CHUNKS = 4
LANES = 128
FINE = 32
MESH = pl.DeviceIdType.MESH


def phase_tables(steps, frequency_values, lag_count):
    lag = np.arange(lag_count, dtype=np.int64) - lag_count // 2
    phase = np.mod(np.asarray(steps, np.int64)[:, None] * lag[None, :], 2 * frequency_values)
    angle = phase.astype(np.float64) * (math.pi / frequency_values)
    return np.stack([np.cos(angle), np.sin(angle)]).astype(np.float32)


def kernel(
    dims,
    raw_ref,
    mask_ref,
    pair_ref,
    rank_table,
    coarse_table,
    fine_table,
    out_ref,
    spec_ref,
    mask_rows,
    held,
    meta,
    slot_smem,
    wide,
    cross_even,
    cross_odd,
    table,
    total,
    from_core,
    to_row,
    from_row,
    local_sem,
    group_send,
    group_recv,
    line_send,
    line_recv,
    meta_send,
    meta_recv,
    meta_line_send,
    meta_line_recv,
    core_send,
    core_recv,
    row_send,
    row_recv,
):
    stations, windows, slots, freqs, lags, groups = dims
    rows = stations * windows * 2
    per_station = windows * 2
    pairs = stations * stations
    held_blocks = GROUP + 2 * REACH
    share = freqs // GROUP
    chunk = share // CHUNKS
    tiles = chunk // LANES

    me = lax.axis_index("sta")
    group = me // GROUP
    rank = me % GROUP
    core = rank % 2
    side = rank // 2
    first = group * GROUP
    has_before = group > 0
    has_behind = group < groups - 1
    before = me - GROUP
    behind = me + GROUP

    barrier = pltpu.get_barrier_semaphore()
    for step in range(1, GROUP):
        pl.semaphore_signal(
            barrier, inc=1, device_id={"sta": first + (rank + step) % GROUP}, device_id_type=MESH
        )

    @pl.when(has_before)
    def _():
        pl.semaphore_signal(barrier, inc=1, device_id={"sta": before}, device_id_type=MESH)

    @pl.when(has_behind)
    def _():
        pl.semaphore_signal(barrier, inc=1, device_id={"sta": behind}, device_id_type=MESH)

    own = REACH + rank
    lane = lax.broadcasted_iota(jnp.int32, (8, LANES), 1)
    slot_row = jnp.zeros((8, LANES), jnp.int32)
    for slot in range(slots):
        for end in range(2):
            slot_row = jnp.where(lane == slot * 2 + end, pair_ref[slot, end], slot_row)
    meta[own, pl.ds(stations, 8), :] = slot_row
    meta[own, pl.ds(0, stations), :] = jnp.zeros((stations, LANES), jnp.int32)
    meta[own, pl.ds(0, stations), pl.ds(0, windows)] = mask_ref[...]

    for w in range(windows):
        valid = jnp.broadcast_to(
            mask_ref[:, pl.ds(w, 1)].astype(jnp.float32), (stations, LANES)
        )
        for part in range(2):
            mask_rows[pl.ds(2 * w + part, stations, stride=per_station), :] = valid

    def mask_part(part, carry):
        valid = mask_rows[...].astype(jnp.bfloat16)
        for tile in range(tiles):
            column = pl.multiple_of(part * chunk + tile * LANES, LANES)
            spec_ref[part, :, pl.ds(tile * LANES, LANES)] = raw_ref[:, pl.ds(column, LANES)] * valid
        return carry

    lax.fori_loop(0, GROUP * CHUNKS, mask_part, 0, unroll=2)

    neighbours = (GROUP - 1) + has_before.astype(jnp.int32) + has_behind.astype(jnp.int32)
    pl.semaphore_wait(barrier, neighbours)

    def group_meta(step):
        return pltpu.make_async_remote_copy(
            src_ref=meta.at[own],
            dst_ref=meta.at[own],
            send_sem=meta_send.at[step - 1],
            recv_sem=meta_recv.at[step - 1],
            device_id={"sta": first + (rank + step) % GROUP},
            device_id_type=MESH,
        )

    def group_copy(index, step):
        peer = (rank + step) % GROUP
        return pltpu.make_async_remote_copy(
            src_ref=spec_ref.at[peer * CHUNKS + index],
            dst_ref=held.at[index, own],
            send_sem=group_send.at[index, step - 1],
            recv_sem=group_recv.at[index, step - 1],
            device_id={"sta": first + peer},
            device_id_type=MESH,
        )

    def own_copy(index):
        return pltpu.make_async_copy(
            spec_ref.at[rank * CHUNKS + index], held.at[index, own], local_sem.at[index]
        )

    def line_copy(index, down):
        source, target, peer = (GROUP, 0, behind) if down else (REACH, GROUP + REACH, before)
        return pltpu.make_async_remote_copy(
            src_ref=held.at[index, pl.ds(source, REACH)],
            dst_ref=held.at[index, pl.ds(target, REACH)],
            send_sem=line_send.at[index, int(down)],
            recv_sem=line_recv.at[index, int(down)],
            device_id={"sta": peer},
            device_id_type=MESH,
        )

    def meta_line(down):
        source, target, peer = (GROUP, 0, behind) if down else (REACH, GROUP + REACH, before)
        return pltpu.make_async_remote_copy(
            src_ref=meta.at[pl.ds(source, REACH)],
            dst_ref=meta.at[pl.ds(target, REACH)],
            send_sem=meta_line_send.at[int(down)],
            recv_sem=meta_line_recv.at[int(down)],
            device_id={"sta": peer},
            device_id_type=MESH,
        )

    steps = (2, 1, 3)
    for step in steps:
        group_meta(step).start()
    for index in range(CHUNKS):
        own_copy(index).start()
        for step in steps:
            group_copy(index, step).start()

    rank_cos = rank_table[0, pl.ds(rank, 1), :]
    rank_sin = rank_table[1, pl.ds(rank, 1), :]

    def fill(index, step, carry):
        coarse = index * (chunk // FINE) + step
        step_cos = coarse_table[0, pl.ds(coarse, 1), :]
        step_sin = coarse_table[1, pl.ds(coarse, 1), :]
        base_cos = step_cos * rank_cos - step_sin * rank_sin
        base_sin = step_sin * rank_cos + step_cos * rank_sin
        row = pl.multiple_of(step * FINE, FINE)
        fine_cos = fine_table[0]
        fine_sin = fine_table[1]
        table[index, pl.ds(row, FINE), :] = (base_cos * fine_cos - base_sin * fine_sin).astype(
            jnp.bfloat16
        )
        table[index, pl.ds(chunk + row, FINE), :] = (
            -(base_sin * fine_cos + base_cos * fine_sin)
        ).astype(jnp.bfloat16)
        return carry

    for index in range(CHUNKS):
        lax.fori_loop(0, chunk // FINE, functools.partial(fill, index), 0)

    def forward(index):
        own_copy(index).wait()
        for step in steps:
            group_copy(index, step).wait_recv()

        @pl.when(has_behind)
        def _():
            line_copy(index, True).start()

        @pl.when(has_before)
        def _():
            line_copy(index, False).start()

    def place(value):
        local = jnp.where(value < 0, REACH, value - (first - REACH))
        return jnp.clip(local, 0, held_blocks - 1)

    half = 2 * slots * pairs
    width = lags // (2 * slots)
    cross_of = (cross_even, cross_odd)

    def product(index, k, column):
        part = jnp.dot(
            cross_of[index % 2][pl.ds(pl.multiple_of(k * half, half), half), :],
            table[index, :, pl.ds(column, width)],
            preferred_element_type=jnp.float32,
        )
        if index > 0:
            part = part + total[k, :, pl.ds(column, width)]
        total[k, :, pl.ds(column, width)] = part

    def work(index):
        @pl.when(has_before)
        def _():
            line_copy(index, True).wait_recv()

        @pl.when(has_behind)
        def _():
            line_copy(index, False).wait_recv()

        def widen(block, carry):
            for tile in range(tiles):
                wide[tile, block] = held[
                    index, block, :, pl.ds(tile * LANES, LANES)
                ].astype(jnp.float32)
            return carry

        lax.fori_loop(0, held_blocks, widen, 0)
        cross = cross_of[index % 2]

        def slot_cross(place_at, carry):
            if index > 0:
                product(
                    index - 1, place_at % 2, pl.multiple_of((place_at // 2) * width, width)
                )
            slot = place_at % slots
            owner = ((place_at // slots) % 2) * 2 + place_at // (2 * slots)
            left = place(slot_smem[owner, 0, slot * 2])
            right = place(slot_smem[owner, 0, slot * 2 + 1])
            out_row = pl.multiple_of(place_at * pairs, pairs)
            for tile in range(tiles):
                column = tile * LANES
                right_real = [
                    wide[tile, right, pl.ds(2 * w, stations, stride=per_station), :]
                    for w in range(windows)
                ]
                right_imag = [
                    wide[tile, right, pl.ds(2 * w + 1, stations, stride=per_station), :]
                    for w in range(windows)
                ]
                for couple in range(0, stations, 2):
                    reals, imags = [], []
                    for station in (couple, couple + 1):
                        real = imag = None
                        for w in range(windows):
                            at = station * per_station + 2 * w
                            left_real = wide[tile, left, pl.ds(at, 1), :]
                            left_imag = wide[tile, left, pl.ds(at + 1, 1), :]
                            real_term = left_real * right_real[w] + left_imag * right_imag[w]
                            imag_term = left_imag * right_real[w] - left_real * right_imag[w]
                            real = real_term if real is None else real + real_term
                            imag = imag_term if imag is None else imag + imag_term
                        reals.append(real)
                        imags.append(imag)
                    at_row = pl.ds(pl.multiple_of(out_row + couple * stations, 16), 16)
                    cross[at_row, pl.ds(column, LANES)] = jnp.concatenate(reals, axis=0).astype(
                        jnp.bfloat16
                    )
                    cross[at_row, pl.ds(chunk + column, LANES)] = jnp.concatenate(
                        imags, axis=0
                    ).astype(jnp.bfloat16)
            return carry

        lax.fori_loop(0, GROUP * slots, slot_cross, 0)

    forward(0)
    for step in steps:
        group_meta(step).wait_recv()
    slots_copy = pltpu.make_async_copy(
        meta.at[pl.ds(REACH, GROUP), pl.ds(stations, 8)], slot_smem, local_sem.at[CHUNKS]
    )
    slots_copy.start()

    @pl.when(has_behind)
    def _():
        meta_line(True).start()

    @pl.when(has_before)
    def _():
        meta_line(False).start()

    slots_copy.wait()

    for index in range(CHUNKS):
        if index + 1 < CHUNKS:
            forward(index + 1)
        work(index)

    mine = slots * pairs
    pieces = lags // width

    def core_copy(piece, to_side):
        column = pl.ds(pl.multiple_of(piece * width, width), width)
        start = pl.multiple_of(to_side * mine, mine)
        return pltpu.make_async_remote_copy(
            src_ref=total.at[1 - core, pl.ds(start, mine), column],
            dst_ref=from_core.at[pl.ds(start, mine), column],
            send_sem=core_send.at[to_side, piece],
            recv_sem=core_recv.at[to_side, piece],
            device_id={"sta": first + side * 2 + 1 - core},
            device_id_type=MESH,
        )

    def row_copy(piece):
        return pltpu.make_async_remote_copy(
            src_ref=to_row.at[piece],
            dst_ref=from_row.at[piece],
            send_sem=row_send.at[piece],
            recv_sem=row_recv.at[piece],
            device_id={"sta": first + (rank + 2) % GROUP},
            device_id_type=MESH,
        )

    def last_of_partner(piece, carry):
        product(CHUNKS - 1, 1 - core, pl.multiple_of(piece * width, width))
        core_copy(piece, 1 - side).start()
        return carry

    lax.fori_loop(0, pieces, last_of_partner, 0)
    for piece in range(pieces):
        core_copy(piece, side).start()
    other = pl.multiple_of((1 - side) * mine, mine)

    def last_of_own(piece, carry):
        column = pl.ds(pl.multiple_of(piece * width, width), width)
        product(CHUNKS - 1, core, pl.multiple_of(piece * width, width))
        core_copy(piece, 1 - side).wait_recv()
        to_row[piece] = (
            total[core, pl.ds(other, mine), column] + from_core[pl.ds(other, mine), column]
        ).astype(jnp.bfloat16)
        row_copy(piece).start()
        return carry

    lax.fori_loop(0, pieces, last_of_own, 0)

    @pl.when(has_before)
    def _():
        meta_line(True).wait_recv()

    @pl.when(has_behind)
    def _():
        meta_line(False).wait_recv()

    scales = []
    for slot in range(slots):
        left_mask = meta[place(pair_ref[slot, 0]), pl.ds(0, stations), :].astype(jnp.float32)
        right_mask = meta[place(pair_ref[slot, 1]), pl.ds(0, stations), :].astype(jnp.float32)
        counts = jnp.concatenate(
            [
                jnp.sum(left_mask[p : p + 1] * right_mask, axis=1, keepdims=True)
                for p in range(stations)
            ],
            axis=0,
        )
        live = jnp.where(pair_ref[slot, 0] >= 0, 1.0, 0.0)
        scales.append(live / (math.sqrt(freqs) * jnp.maximum(counts, 1.0)))

    def finish(piece, carry):
        column = pl.ds(pl.multiple_of(piece * width, width), width)
        core_copy(piece, side).wait_recv()
        row_copy(piece).wait_recv()
        for slot in range(slots):
            start = pl.multiple_of(side * mine + slot * pairs, pairs)
            running = (
                total[core, pl.ds(start, pairs), column]
                + from_core[pl.ds(start, pairs), column]
                + from_row[piece, pl.ds(slot * pairs, pairs), :].astype(jnp.float32)
            )
            out_ref[pl.ds(slot * pairs, pairs), column] = (running * scales[slot]).astype(
                jnp.bfloat16
            )
        return carry

    lax.fori_loop(0, pieces, finish, 0)

    for piece in range(pieces):
        core_copy(piece, side).wait_send()
        core_copy(piece, 1 - side).wait_send()
        row_copy(piece).wait_send()
    for step in steps:
        group_meta(step).wait_send()
        for index in range(CHUNKS):
            group_copy(index, step).wait_send()

    @pl.when(has_behind)
    def _():
        meta_line(True).wait_send()
        for index in range(CHUNKS):
            line_copy(index, True).wait_send()

    @pl.when(has_before)
    def _():
        meta_line(False).wait_send()
        for index in range(CHUNKS):
            line_copy(index, False).wait_send()


def shards(groups, spectra, window_mask, pair_slots):
    stations, windows, _, freqs = spectra.shape
    slots = pair_slots.shape[0]
    rows = stations * windows * 2
    pairs = stations * stations
    held_blocks = GROUP + 2 * REACH
    share = freqs // GROUP
    chunk = share // CHUNKS
    rank_table = phase_tables(np.arange(GROUP) * share, freqs, LAGS)
    coarse_table = phase_tables(np.arange(share // FINE) * FINE, freqs, LAGS)
    fine_table = phase_tables(np.arange(FINE), freqs, LAGS)
    vmem = pl.BlockSpec(memory_space=pltpu.VMEM)
    dma = pltpu.SemaphoreType.DMA
    dims = (stations, windows, slots, freqs, LAGS, groups)
    flops = 2 * GROUP * slots * pairs * 2 * share * LAGS
    out = pl.pallas_call(
        functools.partial(kernel, dims),
        out_shape=jax.ShapeDtypeStruct((slots * pairs, LAGS), jnp.bfloat16),
        in_specs=[vmem, vmem, pl.BlockSpec(memory_space=pltpu.SMEM), vmem, vmem, vmem],
        out_specs=vmem,
        scratch_shapes=[
            pltpu.VMEM((GROUP * CHUNKS, rows, chunk), jnp.bfloat16),
            pltpu.VMEM((rows, LANES), jnp.float32),
            pltpu.VMEM((CHUNKS, held_blocks, rows, chunk), jnp.bfloat16),
            pltpu.VMEM((held_blocks, stations + 8, LANES), jnp.int32),
            pltpu.SMEM((GROUP, 8, LANES), jnp.int32),
            pltpu.VMEM((chunk // LANES, held_blocks, rows, LANES), jnp.float32),
            pltpu.VMEM((GROUP * slots * pairs, 2 * chunk), jnp.bfloat16),
            pltpu.VMEM((GROUP * slots * pairs, 2 * chunk), jnp.bfloat16),
            pltpu.VMEM((CHUNKS, 2 * chunk, LAGS), jnp.bfloat16),
            pltpu.VMEM((2, 2 * slots * pairs, LAGS), jnp.float32),
            pltpu.VMEM((2 * slots * pairs, LAGS), jnp.float32),
            pltpu.VMEM((2 * slots, slots * pairs, LAGS // (2 * slots)), jnp.bfloat16),
            pltpu.VMEM((2 * slots, slots * pairs, LAGS // (2 * slots)), jnp.bfloat16),
            dma((CHUNKS + 1,)),
            dma((CHUNKS, GROUP - 1)),
            dma((CHUNKS, GROUP - 1)),
            dma((CHUNKS, 2)),
            dma((CHUNKS, 2)),
            dma((GROUP - 1,)),
            dma((GROUP - 1,)),
            dma((2,)),
            dma((2,)),
            dma((2, 2 * slots)),
            dma((2, 2 * slots)),
            dma((2 * slots,)),
            dma((2 * slots,)),
        ],
        compiler_params=pltpu.CompilerParams(
            collective_id=0, has_side_effects=True, vmem_limit_bytes=48 * 1024 * 1024
        ),
        cost_estimate=pl.CostEstimate(flops=flops, bytes_accessed=4 * 2**20, transcendentals=0),
    )(
        spectra.reshape(rows, freqs),
        window_mask,
        pair_slots,
        jnp.asarray(rank_table),
        jnp.asarray(coarse_table),
        jnp.asarray(fine_table),
    )
    return out.reshape(slots, stations, stations, LAGS)


def solution(mesh):
    placed = (P(("day", "sta"), None, None, None), P(("day", "sta"), None), P("sta", None))
    groups = mesh.shape["sta"] // GROUP
    return jax.shard_map(
        functools.partial(shards, groups),
        mesh=mesh,
        in_specs=placed,
        out_specs=P(("day", "sta"), None, None, None),
        check_vma=False,
    )
```

```python
import functools
import math

import jax
import jax.numpy as jnp
import numpy as np
from jax import lax
from jax.experimental import pallas as pl
from jax.experimental.pallas import tpu as pltpu
from jax.sharding import PartitionSpec as P

LAGS = 1024
REACH = 2
GROUP = 4
CHUNKS = 4
LANES = 128
FINE = 32
MESH = pl.DeviceIdType.MESH


def phase_tables(steps, frequency_values, lag_count):
    lag = np.arange(lag_count, dtype=np.int64) - lag_count // 2
    phase = np.mod(np.asarray(steps, np.int64)[:, None] * lag[None, :], 2 * frequency_values)
    angle = phase.astype(np.float64) * (math.pi / frequency_values)
    return np.stack([np.cos(angle), np.sin(angle)]).astype(np.float32)


def kernel(
    dims,
    raw_ref,
    mask_ref,
    pair_ref,
    rank_table,
    coarse_table,
    fine_table,
    out_ref,
    spec_ref,
    mask_rows,
    held,
    meta,
    slot_smem,
    wide,
    cross_even,
    cross_odd,
    table,
    total,
    from_core,
    to_row,
    from_row,
    local_sem,
    group_send,
    group_recv,
    line_send,
    line_recv,
    meta_send,
    meta_recv,
    meta_line_send,
    meta_line_recv,
    core_send,
    core_recv,
    row_send,
    row_recv,
):
    stations, windows, slots, freqs, lags, groups = dims
    rows = stations * windows * 2
    per_station = windows * 2
    pairs = stations * stations
    held_blocks = GROUP + 2 * REACH
    share = freqs // GROUP
    chunk = share // CHUNKS
    tiles = chunk // LANES

    me = lax.axis_index("sta")
    group = me // GROUP
    rank = me % GROUP
    core = rank % 2
    side = rank // 2
    first = group * GROUP
    has_before = group > 0
    has_behind = group < groups - 1
    before = me - GROUP
    behind = me + GROUP

    barrier = pltpu.get_barrier_semaphore()
    for step in range(1, GROUP):
        pl.semaphore_signal(
            barrier, inc=1, device_id={"sta": first + (rank + step) % GROUP}, device_id_type=MESH
        )

    @pl.when(has_before)
    def _():
        pl.semaphore_signal(barrier, inc=1, device_id={"sta": before}, device_id_type=MESH)

    @pl.when(has_behind)
    def _():
        pl.semaphore_signal(barrier, inc=1, device_id={"sta": behind}, device_id_type=MESH)

    own = REACH + rank
    lane = lax.broadcasted_iota(jnp.int32, (8, LANES), 1)
    slot_row = jnp.zeros((8, LANES), jnp.int32)
    for slot in range(slots):
        for end in range(2):
            slot_row = jnp.where(lane == slot * 2 + end, pair_ref[slot, end], slot_row)
    meta[own, pl.ds(stations, 8), :] = slot_row
    meta[own, pl.ds(0, stations), :] = jnp.zeros((stations, LANES), jnp.int32)
    meta[own, pl.ds(0, stations), pl.ds(0, windows)] = mask_ref[...]

    for w in range(windows):
        valid = jnp.broadcast_to(
            mask_ref[:, pl.ds(w, 1)].astype(jnp.float32), (stations, LANES)
        )
        for part in range(2):
            mask_rows[pl.ds(2 * w + part, stations, stride=per_station), :] = valid

    def mask_part(part, carry):
        valid = mask_rows[...].astype(jnp.bfloat16)
        for tile in range(tiles):
            column = pl.multiple_of(part * chunk + tile * LANES, LANES)
            spec_ref[part, :, pl.ds(tile * LANES, LANES)] = raw_ref[:, pl.ds(column, LANES)] * valid
        return carry

    lax.fori_loop(0, GROUP * CHUNKS, mask_part, 0, unroll=2)

    neighbours = (GROUP - 1) + has_before.astype(jnp.int32) + has_behind.astype(jnp.int32)
    pl.semaphore_wait(barrier, neighbours)

    def group_meta(step):
        return pltpu.make_async_remote_copy(
            src_ref=meta.at[own],
            dst_ref=meta.at[own],
            send_sem=meta_send.at[step - 1],
            recv_sem=meta_recv.at[step - 1],
            device_id={"sta": first + (rank + step) % GROUP},
            device_id_type=MESH,
        )

    def group_copy(index, step):
        peer = (rank + step) % GROUP
        return pltpu.make_async_remote_copy(
            src_ref=spec_ref.at[peer * CHUNKS + index],
            dst_ref=held.at[index, own],
            send_sem=group_send.at[index, step - 1],
            recv_sem=group_recv.at[index, step - 1],
            device_id={"sta": first + peer},
            device_id_type=MESH,
        )

    def own_copy(index):
        return pltpu.make_async_copy(
            spec_ref.at[rank * CHUNKS + index], held.at[index, own], local_sem.at[index]
        )

    def line_copy(index, down):
        source, target, peer = (GROUP, 0, behind) if down else (REACH, GROUP + REACH, before)
        return pltpu.make_async_remote_copy(
            src_ref=held.at[index, pl.ds(source, REACH)],
            dst_ref=held.at[index, pl.ds(target, REACH)],
            send_sem=line_send.at[index, int(down)],
            recv_sem=line_recv.at[index, int(down)],
            device_id={"sta": peer},
            device_id_type=MESH,
        )

    def meta_line(down):
        source, target, peer = (GROUP, 0, behind) if down else (REACH, GROUP + REACH, before)
        return pltpu.make_async_remote_copy(
            src_ref=meta.at[pl.ds(source, REACH)],
            dst_ref=meta.at[pl.ds(target, REACH)],
            send_sem=meta_line_send.at[int(down)],
            recv_sem=meta_line_recv.at[int(down)],
            device_id={"sta": peer},
            device_id_type=MESH,
        )

    steps = (2, 1, 3)
    for step in steps:
        group_meta(step).start()
    for index in range(CHUNKS):
        own_copy(index).start()
        for step in steps:
            group_copy(index, step).start()

    rank_cos = rank_table[0, pl.ds(rank, 1), :]
    rank_sin = rank_table[1, pl.ds(rank, 1), :]

    def fill(index, step, carry):
        coarse = index * (chunk // FINE) + step
        step_cos = coarse_table[0, pl.ds(coarse, 1), :]
        step_sin = coarse_table[1, pl.ds(coarse, 1), :]
        base_cos = step_cos * rank_cos - step_sin * rank_sin
        base_sin = step_sin * rank_cos + step_cos * rank_sin
        row = pl.multiple_of(step * FINE, FINE)
        fine_cos = fine_table[0]
        fine_sin = fine_table[1]
        table[index, pl.ds(row, FINE), :] = (base_cos * fine_cos - base_sin * fine_sin).astype(
            jnp.bfloat16
        )
        table[index, pl.ds(chunk + row, FINE), :] = (
            -(base_sin * fine_cos + base_cos * fine_sin)
        ).astype(jnp.bfloat16)
        return carry

    for index in range(CHUNKS):
        lax.fori_loop(0, chunk // FINE, functools.partial(fill, index), 0)

    def forward(index):
        own_copy(index).wait()
        for step in steps:
            group_copy(index, step).wait_recv()

        @pl.when(has_behind)
        def _():
            line_copy(index, True).start()

        @pl.when(has_before)
        def _():
            line_copy(index, False).start()

    def place(value):
        local = jnp.where(value < 0, REACH, value - (first - REACH))
        return jnp.clip(local, 0, held_blocks - 1)

    half = 2 * slots * pairs
    width = lags // (2 * slots)
    cross_of = (cross_even, cross_odd)

    def product(index, k, column):
        part = jnp.dot(
            cross_of[index % 2][pl.ds(pl.multiple_of(k * half, half), half), :],
            table[index, :, pl.ds(column, width)],
            preferred_element_type=jnp.float32,
        )
        if index > 0:
            part = part + total[k, :, pl.ds(column, width)]
        total[k, :, pl.ds(column, width)] = part

    def work(index):
        @pl.when(has_before)
        def _():
            line_copy(index, True).wait_recv()

        @pl.when(has_behind)
        def _():
            line_copy(index, False).wait_recv()

        def widen(block, carry):
            for tile in range(tiles):
                wide[tile, block] = held[
                    index, block, :, pl.ds(tile * LANES, LANES)
                ].astype(jnp.float32)
            return carry

        lax.fori_loop(0, held_blocks, widen, 0)
        cross = cross_of[index % 2]

        def slot_cross(place_at):
            slot = place_at % slots
            owner = ((place_at // slots) % 2) * 2 + place_at // (2 * slots)
            left = place(slot_smem[owner, 0, slot * 2])
            right = place(slot_smem[owner, 0, slot * 2 + 1])
            out_row = pl.multiple_of(place_at * pairs, pairs)
            for tile in range(tiles):
                column = tile * LANES
                right_real = [
                    wide[tile, right, pl.ds(2 * w, stations, stride=per_station), :]
                    for w in range(windows)
                ]
                right_imag = [
                    wide[tile, right, pl.ds(2 * w + 1, stations, stride=per_station), :]
                    for w in range(windows)
                ]
                for couple in range(0, stations, 2):
                    reals, imags = [], []
                    for station in (couple, couple + 1):
                        real = imag = None
                        for w in range(windows):
                            at = station * per_station + 2 * w
                            left_real = wide[tile, left, pl.ds(at, 1), :]
                            left_imag = wide[tile, left, pl.ds(at + 1, 1), :]
                            real_term = left_real * right_real[w] + left_imag * right_imag[w]
                            imag_term = left_imag * right_real[w] - left_real * right_imag[w]
                            real = real_term if real is None else real + real_term
                            imag = imag_term if imag is None else imag + imag_term
                        reals.append(real)
                        imags.append(imag)
                    at_row = pl.ds(pl.multiple_of(out_row + couple * stations, 16), 16)
                    cross[at_row, pl.ds(column, LANES)] = jnp.concatenate(reals, axis=0).astype(
                        jnp.bfloat16
                    )
                    cross[at_row, pl.ds(chunk + column, LANES)] = jnp.concatenate(
                        imags, axis=0
                    ).astype(jnp.bfloat16)

        def columns_and_slots(piece, carry):
            if index > 0:
                column = pl.ds(pl.multiple_of(piece * width, width), width)
                part = jnp.dot(
                    cross_of[(index - 1) % 2][...],
                    table[index - 1, :, column],
                    preferred_element_type=jnp.float32,
                )
                for k in range(2):
                    rows_of = part[k * half : (k + 1) * half]
                    if index > 1:
                        rows_of = rows_of + total[k, :, column]
                    total[k, :, column] = rows_of
            slot_cross(piece * 2)
            slot_cross(piece * 2 + 1)
            return carry

        lax.fori_loop(0, GROUP * slots // 2, columns_and_slots, 0)

    forward(0)
    for step in steps:
        group_meta(step).wait_recv()
    slots_copy = pltpu.make_async_copy(
        meta.at[pl.ds(REACH, GROUP), pl.ds(stations, 8)], slot_smem, local_sem.at[CHUNKS]
    )
    slots_copy.start()

    @pl.when(has_behind)
    def _():
        meta_line(True).start()

    @pl.when(has_before)
    def _():
        meta_line(False).start()

    slots_copy.wait()

    for index in range(CHUNKS):
        if index + 1 < CHUNKS:
            forward(index + 1)
        work(index)

    mine = slots * pairs
    pieces = lags // width

    def core_copy(piece, to_side):
        column = pl.ds(pl.multiple_of(piece * width, width), width)
        start = pl.multiple_of(to_side * mine, mine)
        return pltpu.make_async_remote_copy(
            src_ref=total.at[1 - core, pl.ds(start, mine), column],
            dst_ref=from_core.at[pl.ds(start, mine), column],
            send_sem=core_send.at[to_side, piece],
            recv_sem=core_recv.at[to_side, piece],
            device_id={"sta": first + side * 2 + 1 - core},
            device_id_type=MESH,
        )

    def row_copy(piece):
        return pltpu.make_async_remote_copy(
            src_ref=to_row.at[piece],
            dst_ref=from_row.at[piece],
            send_sem=row_send.at[piece],
            recv_sem=row_recv.at[piece],
            device_id={"sta": first + (rank + 2) % GROUP},
            device_id_type=MESH,
        )

    def last_of_partner(piece, carry):
        product(CHUNKS - 1, 1 - core, pl.multiple_of(piece * width, width))
        core_copy(piece, 1 - side).start()
        return carry

    lax.fori_loop(0, pieces, last_of_partner, 0)
    for piece in range(pieces):
        core_copy(piece, side).start()
    other = pl.multiple_of((1 - side) * mine, mine)

    def last_of_own(piece, carry):
        column = pl.ds(pl.multiple_of(piece * width, width), width)
        product(CHUNKS - 1, core, pl.multiple_of(piece * width, width))
        core_copy(piece, 1 - side).wait_recv()
        to_row[piece] = (
            total[core, pl.ds(other, mine), column] + from_core[pl.ds(other, mine), column]
        ).astype(jnp.bfloat16)
        row_copy(piece).start()
        return carry

    lax.fori_loop(0, pieces, last_of_own, 0)

    @pl.when(has_before)
    def _():
        meta_line(True).wait_recv()

    @pl.when(has_behind)
    def _():
        meta_line(False).wait_recv()

    scales = []
    for slot in range(slots):
        left_mask = meta[place(pair_ref[slot, 0]), pl.ds(0, stations), :].astype(jnp.float32)
        right_mask = meta[place(pair_ref[slot, 1]), pl.ds(0, stations), :].astype(jnp.float32)
        counts = jnp.concatenate(
            [
                jnp.sum(left_mask[p : p + 1] * right_mask, axis=1, keepdims=True)
                for p in range(stations)
            ],
            axis=0,
        )
        live = jnp.where(pair_ref[slot, 0] >= 0, 1.0, 0.0)
        scales.append(live / (math.sqrt(freqs) * jnp.maximum(counts, 1.0)))

    def finish(piece, carry):
        column = pl.ds(pl.multiple_of(piece * width, width), width)
        core_copy(piece, side).wait_recv()
        row_copy(piece).wait_recv()
        for slot in range(slots):
            start = pl.multiple_of(side * mine + slot * pairs, pairs)
            running = (
                total[core, pl.ds(start, pairs), column]
                + from_core[pl.ds(start, pairs), column]
                + from_row[piece, pl.ds(slot * pairs, pairs), :].astype(jnp.float32)
            )
            out_ref[pl.ds(slot * pairs, pairs), column] = (running * scales[slot]).astype(
                jnp.bfloat16
            )
        return carry

    lax.fori_loop(0, pieces, finish, 0)

    for piece in range(pieces):
        core_copy(piece, side).wait_send()
        core_copy(piece, 1 - side).wait_send()
        row_copy(piece).wait_send()
    for step in steps:
        group_meta(step).wait_send()
        for index in range(CHUNKS):
            group_copy(index, step).wait_send()

    @pl.when(has_behind)
    def _():
        meta_line(True).wait_send()
        for index in range(CHUNKS):
            line_copy(index, True).wait_send()

    @pl.when(has_before)
    def _():
        meta_line(False).wait_send()
        for index in range(CHUNKS):
            line_copy(index, False).wait_send()


def shards(groups, spectra, window_mask, pair_slots):
    stations, windows, _, freqs = spectra.shape
    slots = pair_slots.shape[0]
    rows = stations * windows * 2
    pairs = stations * stations
    held_blocks = GROUP + 2 * REACH
    share = freqs // GROUP
    chunk = share // CHUNKS
    rank_table = phase_tables(np.arange(GROUP) * share, freqs, LAGS)
    coarse_table = phase_tables(np.arange(share // FINE) * FINE, freqs, LAGS)
    fine_table = phase_tables(np.arange(FINE), freqs, LAGS)
    vmem = pl.BlockSpec(memory_space=pltpu.VMEM)
    dma = pltpu.SemaphoreType.DMA
    dims = (stations, windows, slots, freqs, LAGS, groups)
    flops = 2 * GROUP * slots * pairs * 2 * share * LAGS
    out = pl.pallas_call(
        functools.partial(kernel, dims),
        out_shape=jax.ShapeDtypeStruct((slots * pairs, LAGS), jnp.bfloat16),
        in_specs=[vmem, vmem, pl.BlockSpec(memory_space=pltpu.SMEM), vmem, vmem, vmem],
        out_specs=vmem,
        scratch_shapes=[
            pltpu.VMEM((GROUP * CHUNKS, rows, chunk), jnp.bfloat16),
            pltpu.VMEM((rows, LANES), jnp.float32),
            pltpu.VMEM((CHUNKS, held_blocks, rows, chunk), jnp.bfloat16),
            pltpu.VMEM((held_blocks, stations + 8, LANES), jnp.int32),
            pltpu.SMEM((GROUP, 8, LANES), jnp.int32),
            pltpu.VMEM((chunk // LANES, held_blocks, rows, LANES), jnp.float32),
            pltpu.VMEM((GROUP * slots * pairs, 2 * chunk), jnp.bfloat16),
            pltpu.VMEM((GROUP * slots * pairs, 2 * chunk), jnp.bfloat16),
            pltpu.VMEM((CHUNKS, 2 * chunk, LAGS), jnp.bfloat16),
            pltpu.VMEM((2, 2 * slots * pairs, LAGS), jnp.float32),
            pltpu.VMEM((2 * slots * pairs, LAGS), jnp.float32),
            pltpu.VMEM((2 * slots, slots * pairs, LAGS // (2 * slots)), jnp.bfloat16),
            pltpu.VMEM((2 * slots, slots * pairs, LAGS // (2 * slots)), jnp.bfloat16),
            dma((CHUNKS + 1,)),
            dma((CHUNKS, GROUP - 1)),
            dma((CHUNKS, GROUP - 1)),
            dma((CHUNKS, 2)),
            dma((CHUNKS, 2)),
            dma((GROUP - 1,)),
            dma((GROUP - 1,)),
            dma((2,)),
            dma((2,)),
            dma((2, 2 * slots)),
            dma((2, 2 * slots)),
            dma((2 * slots,)),
            dma((2 * slots,)),
        ],
        compiler_params=pltpu.CompilerParams(
            collective_id=0, has_side_effects=True, vmem_limit_bytes=48 * 1024 * 1024
        ),
        cost_estimate=pl.CostEstimate(flops=flops, bytes_accessed=4 * 2**20, transcendentals=0),
    )(
        spectra.reshape(rows, freqs),
        window_mask,
        pair_slots,
        jnp.asarray(rank_table),
        jnp.asarray(coarse_table),
        jnp.asarray(fine_table),
    )
    return out.reshape(slots, stations, stations, LAGS)


def solution(mesh):
    placed = (P(("day", "sta"), None, None, None), P(("day", "sta"), None), P("sta", None))
    groups = mesh.shape["sta"] // GROUP
    return jax.shard_map(
        functools.partial(shards, groups),
        mesh=mesh,
        in_specs=placed,
        out_specs=P(("day", "sta"), None, None, None),
        check_vma=False,
    )
```
